128 devices in a mesh: dp: 32 (over z, x, y_hi), mp: 4 (over y_lo, core).
Axes of the slice: x: 4, y: 4 (y_hi: 2, y_lo: 2; y = y_hi * 2 + y_lo), z: 4, core: 2. Of those that a mesh axis runs over, the one named last changes fastest.
Arguments:
- image_pool: bfloat16 [32768, 1152], P(('dp', 'mp')), may hold values from -6 to 6
- text_pool: bfloat16 [32768, 1152], P(('dp', 'mp')), may hold values from -6 to 6
- image_head: bfloat16 [1152, 1152], P(None, 'mp'), may hold values from -0.1875 to 0.1875
- text_head: bfloat16 [1152, 1152], P(None, 'mp'), may hold values from -0.1875 to 0.1875
- logit_scale: float32 [1], replicated, may hold values from 8 to 12
- logit_bias: float32 [1], replicated, may hold values from -1.5 to -0.5
Outputs:
- grad_image: bfloat16 [32768, 1152], P(('dp', 'mp'))
- grad_text: bfloat16 [32768, 1152], P(('dp', 'mp'))
- grad_image_head: float32 [1152, 1152], P(None, 'mp')
- grad_text_head: float32 [1152, 1152], P(None, 'mp')
The draws below stay inside these ranges and needn't reach their ends.
All inputs are finite; a program needn't handle non-finite values.
Results may differ from the reference program's by a relative error of at most 0.008.
Values may be sent and summed in bfloat16 or wider, within the bound.
No kernel may reach another device: no remote copies, remote signals or barrier semaphores. Data moves between devices by JAX's collectives and lax.ppermute only.
A program may use at most 128 MiB of HBM per device.

```python
import jax
import jax.numpy as jnp
from jax import lax

D = 1152
IMG_DEV = 256
WIN = 4
BATCH = 32768
N_DP = 32
N_MP = 4


def block_levels(key, shape, split, low, largest):
    gain, own = 1.0, jax.random.fold_in(key, 6)
    for axis_at, blocks in split:
        steps = jnp.exp(jax.random.uniform(jax.random.fold_in(own, axis_at), (blocks,), jnp.float32, low / len(split), largest / len(split)))
        gain = gain * jnp.repeat(steps, shape[axis_at] // blocks).reshape([-1 if axis == axis_at else 1 for axis in range(len(shape))])
    return gain


def scatter_about(rng, dims, width, bound, shards=(), kind=jnp.bfloat16):
    values = width * jax.random.normal(rng, dims, jnp.float32)
    if shards:
        values = values * block_levels(rng, dims, shards, -0.22, 0.18)
    return jnp.clip(values, -bound, bound).astype(kind)


def setup_inputs(seed: int = 0) -> dict:
    key_of = jax.random.split(jax.random.key(seed), 7)
    image_pool = scatter_about(key_of[0], (BATCH, D), 1.0, 6.0, ((0, 128),))
    text_pool = scatter_about(key_of[1], (BATCH, D), 1.0, 6.0, ((0, 128),))
    image_head = scatter_about(key_of[2], (D, D), D ** -0.5, 0.1875, ((1, 4),))
    text_head = scatter_about(key_of[3], (D, D), D ** -0.5, 0.1875, ((1, 4),))
    logit_scale = jnp.clip(jax.random.uniform(key_of[4], (1,), jnp.float32, 8.0, 12.0), 8.0, 12.0)
    logit_bias = jnp.clip(jax.random.uniform(key_of[5], (1,), jnp.float32, -1.5, -0.5), -1.5, -0.5)
    return dict(image_pool=image_pool, text_pool=text_pool, image_head=image_head, text_head=text_head, logit_scale=logit_scale, logit_bias=logit_bias)


def embed(pooled, head):
    raw = jnp.dot(pooled, head, preferred_element_type=jnp.float32)
    inverse = lax.rsqrt(lax.optimization_barrier(jnp.sum(raw * raw, axis=1, keepdims=True)) + 1e-06)
    return (raw * inverse, inverse)

def unembed(grads, unit, inverse):
    inner = lax.optimization_barrier(jnp.sum(unit * grads, axis=1, keepdims=True))
    return ((grads - unit * inner) * inverse).astype(jnp.bfloat16)

def reference(image_pool, text_pool, image_head, text_head, logit_scale, logit_bias):
    image_unit, image_inv = embed(image_pool, image_head)
    text_unit, text_inv = embed(text_pool, text_head)
    block = IMG_DEV * N_MP
    image_blocks = image_unit.astype(jnp.bfloat16).astype(jnp.float32).reshape(N_DP, block, D)
    text_blocks = text_unit.astype(jnp.bfloat16).astype(jnp.float32).reshape(N_DP, block, D)
    scale = logit_scale[0]
    bias = logit_bias[0]
    weight_c = 1.0 / (WIN * block)
    labels = jnp.eye(block, dtype=jnp.float32)
    grad_x = jnp.zeros((N_DP, block, D), jnp.float32)
    grad_y = jnp.zeros((N_DP, block, D), jnp.float32)
    for step in range(WIN):
        moved = jnp.roll(text_blocks, step, axis=0)
        score = scale * jnp.einsum('bik,bjk->bij', image_blocks, moved) + bias
        target = labels if step == 0 else jnp.zeros_like(labels)
        tile = lax.optimization_barrier((weight_c * (jax.nn.sigmoid(score) - target)).astype(jnp.bfloat16))
        tile = tile.astype(jnp.float32)
        grad_x = grad_x + scale * jnp.einsum('bij,bjk->bik', tile, moved)
        grad_y = grad_y + jnp.roll(scale * jnp.einsum('bij,bik->bjk', tile, image_blocks), -step, axis=0)
    raw_image = unembed(grad_x.reshape(BATCH, D), image_unit, image_inv)
    raw_text = unembed(grad_y.reshape(BATCH, D), text_unit, text_inv)
    grad_image = jnp.dot(raw_image, image_head.T, preferred_element_type=jnp.float32).astype(jnp.bfloat16)
    grad_text = jnp.dot(raw_text, text_head.T, preferred_element_type=jnp.float32).astype(jnp.bfloat16)
    grad_image_head = jnp.dot(image_pool.T, raw_image, preferred_element_type=jnp.float32)
    grad_text_head = jnp.dot(text_pool.T, raw_text, preferred_element_type=jnp.float32)
    return (grad_image, grad_text, grad_image_head, grad_text_head)
```

```python
import jax
import jax.numpy as jnp
from jax import lax
from jax.sharding import Mesh, PartitionSpec as P

WIN = 4
AXES = ("z", "x", "yh", "yl", "core")
SIZES = (4, 4, 2, 2, 2)
BF = jnp.bfloat16
F32 = jnp.float32


def flat(z, x, y, core):
    return (((z % 4) * 4 + x % 4) * 4 + y % 4) * 2 + core


def moved(block, route):
    pairs = []
    for z in range(4):
        for x in range(4):
            for y in range(4):
                for core in range(2):
                    place = route(z, x, y, core)
                    if place is not None:
                        pairs.append((flat(z, x, y, core), flat(*place)))
    return lax.ppermute(block, AXES, pairs)


def hop(dz=0, dx=0, dy=0, swap=0):
    return lambda z, x, y, core: (z + dz, x + dx, y + dy, core ^ swap)


def collect(step, parity=None, direct=False):
    def route(z, x, y, core):
        role = core ^ 1 if direct else core
        if role:
            z, x, y = 3 - z, 3 - x, 3 - y
        column, odd, half = z * 4 + x, y // 2, y % 2
        if parity is not None and odd != parity:
            return None
        if step == "half":
            half = 1 - half
        elif step == "column":
            column = (column + 1) % 16
        elif step == "cross":
            odd, half = 1 - odd, 1 - half
        z, x, y = column // 4, column % 4, odd * 2 + half
        if role:
            z, x, y = 3 - z, 3 - x, 3 - y
        return (z, x, y, role)

    return route


def dot_nt(left, right):
    return lax.dot_general(
        left, right, (((1,), (1,)), ((), ())), preferred_element_type=F32
    )


def dot_nn(left, right):
    return jnp.dot(left, right, preferred_element_type=F32)


def body(image_pool, text_pool, image_head, text_head, logit_scale, logit_bias):
    core = lax.axis_index("core")
    half = lax.axis_index("yl")
    odd = lax.axis_index("yh")
    plane = lax.axis_index("z")
    first = core == 0
    scale = logit_scale[0]
    bias = logit_bias[0]
    rows, width = image_pool.shape
    columns = image_head.shape[1]
    weight_c = 1.0 / (WIN * 4 * rows)

    head_own = jnp.where(first, image_head, text_head).T
    head_other = jnp.where(first, text_head, image_head).T
    pool_own = jnp.where(first, image_pool, text_pool)
    pool_other = jnp.where(first, text_pool, image_pool)
    head_up = moved(head_own, hop(dy=1))
    head_down = moved(head_other, hop(dy=-1, swap=1))
    head_mate = moved(head_other, hop(swap=1))
    pool_mate = moved(pool_other, hop(swap=1))
    pool = jnp.concatenate([pool_own, pool_mate], axis=0)
    head = jnp.zeros((4 * columns, width), BF)
    far = 1 - half
    for part, place in (
        (head_own, 2 * half + core),
        (head_mate, 2 * half + 1 - core),
        (head_up, 2 * far + core),
        (head_down, 2 * far + 1 - core),
    ):
        head = lax.dynamic_update_slice(head, part, (place * columns, 0))

    raw = dot_nt(pool, head)
    inverse = lax.rsqrt(jnp.sum(raw * raw, axis=1, keepdims=True) + 1e-06)
    unit = raw * inverse
    emb = unit.astype(BF)

    pool_z1 = moved(pool, hop(dz=1))
    pool_z3 = moved(pool, hop(dz=-1))

    count = 2 * rows
    ids = lax.broadcasted_iota(jnp.int32, (count, count), 0)
    jds = lax.broadcasted_iota(jnp.int32, (count, count), 1)
    label = (ids == (jds + rows) % count).astype(F32)

    def term(other, target=0.0):
        score = scale * dot_nt(emb, other) + bias
        tile = (weight_c * (jax.nn.sigmoid(score) - target)).astype(BF)
        return dot_nn(tile, other)

    b0n = moved(emb, collect("same", direct=True))
    b2n = moved(emb, collect("column", direct=True))
    c1a = moved(emb, collect("cross", parity=0, direct=True))
    b0f = moved(emb, collect("half", direct=True))
    grad = term(b0n, label)
    grad = grad + term(b2n)
    c1b = moved(b2n, collect("cross", parity=1))
    x3o = moved(c1a, collect("column", parity=1))
    b2f = moved(b0f, collect("column"))
    c2a = moved(b0f, collect("cross", parity=0))
    grad = grad + term(b0f)
    is_odd = jnp.where(first, odd, 1 - odd) == 1
    b1f = jnp.where(is_odd, c1a, c1b)
    x3e = moved(c1b, collect("column", parity=0))
    grad = grad + term(b1f)
    c2b = moved(b2f, collect("cross", parity=1))
    grad = grad + term(b2f)
    b3f = jnp.where(is_odd, x3o, x3e)
    b3n = moved(b3f, collect("half"))
    grad = grad + term(b3f)
    b1n = jnp.where(is_odd, c2a, c2b)
    grad = grad + term(b1n)
    pool_late, b3f = lax.optimization_barrier((pool, b3f))
    pool_z2 = moved(pool_late, hop(dz=2))
    grad = scale * (grad + term(b3n))

    inner = jnp.sum(unit * grad, axis=1, keepdims=True)
    raw_grad = ((grad - unit * inner) * inverse).astype(BF)

    piece = columns // 4
    turned = raw_grad.T.reshape(4, 4, piece, count)

    def slice_of(place):
        return lax.dynamic_index_in_dim(turned, place % 4, 1, False).reshape(columns, count)

    part1 = moved(slice_of(plane + 1), hop(dz=1))
    part3 = moved(slice_of(plane + 3), hop(dz=-1))
    part2 = moved(slice_of(plane + 2), hop(dz=2))
    grad_pool = dot_nn(raw_grad, head).astype(BF)
    pool_back = moved(grad_pool[rows:], hop(swap=1))
    grad_image = jnp.where(first, grad_pool[:rows], pool_back)
    grad_text = jnp.where(first, pool_back, grad_pool[:rows])
    total = dot_nn(slice_of(plane), pool) + dot_nn(part1, pool_z1)
    total = total + dot_nn(part3, pool_z3) + dot_nn(part2, pool_z2)
    total = total.reshape(4, piece, width)

    def shard_for(yh, yl):
        return lax.dynamic_index_in_dim(total, 2 * yl + yh, 0, False)

    up_h = jnp.where(half == 1, 1 - odd, odd)
    down_h = jnp.where(half == 0, 1 - odd, odd)
    got = [
        moved(shard_for(up_h, 1 - half).astype(BF), hop(dy=1)),
        moved(shard_for(down_h, 1 - half).astype(BF), hop(dy=-1)),
        moved(shard_for(1 - odd, half).astype(BF), hop(dy=2)),
    ]
    mine = shard_for(odd, half)
    for part in got:
        mine = mine + part.astype(F32)
    narrow = mine.astype(BF)
    for part in [moved(narrow, hop(dx=1)), moved(narrow, hop(dx=-1)), moved(narrow, hop(dx=2))]:
        mine = mine + part.astype(F32)
    narrow = mine.astype(BF)
    across = moved(narrow, hop(dy=2))
    low = jnp.where(odd == 0, narrow, across)
    high = jnp.where(odd == 0, across, narrow)
    pair = jnp.stack([low, high])
    ring = [pair, moved(pair, hop(dz=-1)), moved(pair, hop(dz=2)), moved(pair, hop(dz=1))]
    ring = jnp.stack(ring + ring, axis=1)
    ring = lax.dynamic_slice_in_dim(ring, 4 - plane, 4, 1)
    ring = ring.reshape(2, columns, width)
    keep = lax.dynamic_index_in_dim(ring, core, 0, False)
    give = lax.dynamic_index_in_dim(ring, 1 - core, 0, False)
    back = moved(give, hop(swap=1))
    head_image = jnp.where(first, keep, back).astype(F32).T
    head_text = jnp.where(first, back, keep).astype(F32).T
    return (grad_image, grad_text, head_image, head_text)


def solution(mesh):
    fine = Mesh(mesh.devices.reshape(SIZES), AXES)
    rows = P(AXES, None)
    cols = P(None, ("yl", "core"))
    return jax.shard_map(
        body,
        mesh=fine,
        in_specs=(rows, rows, cols, cols, P(), P()),
        out_specs=(rows, rows, cols, cols),
        check_vma=False,
    )
```

```python
import functools

import jax
import jax.numpy as jnp
from jax import lax
from jax.experimental import pallas as pl
from jax.experimental.pallas import tpu as pltpu
from jax.sharding import Mesh, PartitionSpec as P

WIN = 4
COST = 10**6
VMEM = 40 * 2**20
AXES = ("z", "x", "yh", "yl", "core")
SIZES = (4, 4, 2, 2, 2)
BF = jnp.bfloat16
F32 = jnp.float32


def flat(z, x, y, core):
    return (((z % 4) * 4 + x % 4) * 4 + y % 4) * 2 + core


def moved(block, route):
    pairs = []
    for z in range(4):
        for x in range(4):
            for y in range(4):
                for core in range(2):
                    place = route(z, x, y, core)
                    if place is not None:
                        pairs.append((flat(z, x, y, core), flat(*place)))
    return lax.ppermute(block, AXES, pairs)


def hop(dz=0, dx=0, dy=0, swap=0):
    return lambda z, x, y, core: (z + dz, x + dx, y + dy, core ^ swap)


def collect(step, parity=None, direct=False):
    def route(z, x, y, core):
        role = core ^ 1 if direct else core
        if role:
            z, x, y = 3 - z, 3 - x, 3 - y
        column, odd, half = z * 4 + x, y // 2, y % 2
        if parity is not None and odd != parity:
            return None
        if step == "half":
            half = 1 - half
        elif step == "column":
            column = (column + 1) % 16
        elif step == "cross":
            odd, half = 1 - odd, 1 - half
        z, x, y = column // 4, column % 4, odd * 2 + half
        if role:
            z, x, y = 3 - z, 3 - x, 3 - y
        return (z, x, y, role)

    return route


def after(value, *others):
    return lax.optimization_barrier((value,) + others)[0]


def dot_nt(left, right):
    return lax.dot_general(
        left, right, (((1,), (1,)), ((), ())), preferred_element_type=F32
    )


def dot_nn(left, right):
    return jnp.dot(left, right, preferred_element_type=F32)


def embed_kernel(place, own, mate, *refs):
    parts, (unit, emb, inverse, head, sem) = refs[:4], refs[4:]
    columns = parts[0].shape[0]
    copies = []
    for i, part in enumerate(parts):
        start = pl.multiple_of(place[i] * columns, 16)
        copies.append(pltpu.make_async_copy(part, head.at[pl.ds(start, columns)], sem.at[i]))
    for copy in copies:
        copy.start()
    for copy in copies:
        copy.wait()
    rows = own.shape[0]
    for at, pool in ((0, own), (rows, mate)):
        raw = dot_nt(pool[...], head[...])
        norm = lax.rsqrt(jnp.sum(raw * raw, axis=1, keepdims=True) + 1e-06)
        raw = raw * norm
        inverse[at : at + rows, :] = norm
        unit[at : at + rows, :] = raw
        emb[at : at + rows, :] = raw.astype(BF)


def embed(own, mate, parts, place):
    rows, width = own.shape
    vmem = pl.BlockSpec(memory_space=pltpu.VMEM)
    return pl.pallas_call(
        embed_kernel,
        in_specs=[pl.BlockSpec(memory_space=pltpu.SMEM), vmem, vmem]
        + [pl.BlockSpec(memory_space=pl.ANY)] * 4,
        out_specs=[vmem] * 4,
        out_shape=[
            jax.ShapeDtypeStruct((2 * rows, width), F32),
            jax.ShapeDtypeStruct((2 * rows, width), BF),
            jax.ShapeDtypeStruct((2 * rows, 1), F32),
            jax.ShapeDtypeStruct((width, width), BF),
        ],
        scratch_shapes=[pltpu.SemaphoreType.DMA((4,))],
        compiler_params=pltpu.CompilerParams(vmem_limit_bytes=VMEM),
        cost_estimate=pl.CostEstimate(flops=COST, bytes_accessed=2**20, transcendentals=0),
        name="embed",
    )(place, own, mate, *parts)


def sums_kernel(plan, *refs):
    names, units, label = plan
    ref = dict(zip(names, refs))
    scale, bias = ref["scale"][0], ref["bias"][0]
    step = pl.program_id(0)
    copies = {}
    for place, unit in enumerate(units):
        if isinstance(unit, tuple):
            copies[place] = [
                pltpu.make_async_copy(ref[name], ref["held"].at[place], ref["sem"].at[place])
                for name in unit
            ]
            for copy, parity in zip(copies[place], (1, 0)):
                pl.when((step == 0) & (ref["odd"][0] == parity))(copy.start)

    emb = ref["emb"][...]
    rows = emb.shape[0]
    total = ref["sum"][...] if "sum" in ref else None
    for place, unit in enumerate(units):
        if place in copies:
            pl.when(step == 0)(copies[place][0].wait)
        block = ref["held"][place] if isinstance(unit, tuple) else ref[unit][...]
        count = block.shape[0]
        score = scale * dot_nt(emb, block) + bias
        below = 1.0 + jnp.exp(-score)
        tile = pl.reciprocal(below, approx=True)
        tile = tile * (2.0 - below * tile)
        if label and place == 0:
            ids = lax.broadcasted_iota(jnp.int32, score.shape, 0) + step * rows
            jds = lax.broadcasted_iota(jnp.int32, score.shape, 1)
            shift = jnp.where(jds < count // 2, count // 2, -(count // 2))
            tile = tile - (ids == jds + shift).astype(F32)
        tile = (tile * (1.0 / (WIN * 2 * count))).astype(BF)
        term = dot_nn(tile, block)
        total = term if total is None else total + term
    if "raw" not in ref:
        ref["out"][...] = total
        return
    unit, inverse = ref["unit"][...], ref["inverse"][...]
    grad = total * scale
    inner = jnp.sum(unit * grad, axis=1, keepdims=True)
    raw = (grad - unit * inner) * inverse
    ref["raw"][...] = raw.astype(BF)
    ref["turned"][...] = raw.T
    piece = ref["to0"].shape[0] // 4
    for ahead in range(4):
        parts = []
        for shard in range(4):
            start = pl.multiple_of(ref["order"][ahead * 4 + shard] * piece, 8)
            parts.append(ref["turned"][pl.ds(start, piece), :])
        ref["to%d" % ahead][...] = jnp.concatenate(parts, axis=0).astype(BF)


def sums(emb, units, scale, bias, odd, total=None, label=False, finish=None):
    count, width = emb.shape
    block = 256
    smem = pl.BlockSpec(memory_space=pltpu.SMEM)
    rows = pl.BlockSpec((block, width), lambda i: (i, 0))
    whole = pl.BlockSpec((count, width), lambda i: (0, 0))
    names, args, specs = ["scale", "bias", "odd", "emb"], [scale, bias, odd, emb], [smem] * 3 + [rows]
    plan = []
    for place, unit in enumerate(units):
        if isinstance(unit, tuple):
            pair = ("a%d" % place, "b%d" % place)
            plan.append(pair)
            names += pair
            args += unit
            specs += [pl.BlockSpec(memory_space=pl.ANY)] * 2
        else:
            plan.append("u%d" % place)
            names.append("u%d" % place)
            args.append(unit)
            specs.append(whole)
    if total is not None:
        names.append("sum")
        args.append(total)
        specs.append(rows)
    if finish is None:
        outs = [("out", (count, width), F32, rows)]
    else:
        unit, inverse, order = finish
        names += ["unit", "inverse", "order"]
        args += [unit, inverse, order]
        specs += [rows, pl.BlockSpec((block, 1), lambda i: (i, 0)), smem]
        outs = [("raw", (count, width), BF, rows)]
        part = pl.BlockSpec((width // 4, block), lambda i: (0, i))
        outs += [("to%d" % i, (width // 4, count), BF, part) for i in range(4)]
    names += [out[0] for out in outs]
    scratch = []
    if any(isinstance(unit, tuple) for unit in units):
        names += ["held", "sem"]
        scratch += [
            pltpu.VMEM((len(units), count, width), BF),
            pltpu.SemaphoreType.DMA((len(units),)),
        ]
    if finish is not None:
        names.append("turned")
        scratch.append(pltpu.VMEM((width, block), F32))
    result = pl.pallas_call(
        functools.partial(sums_kernel, (tuple(names), tuple(plan), label)),
        grid=(count // block,),
        in_specs=specs,
        out_specs=[out[3] for out in outs],
        out_shape=[jax.ShapeDtypeStruct(out[1], out[2]) for out in outs],
        scratch_shapes=scratch,
        compiler_params=pltpu.CompilerParams(vmem_limit_bytes=VMEM),
        cost_estimate=pl.CostEstimate(flops=COST, bytes_accessed=2**20, transcendentals=0),
        name="finish" if finish is not None else "sums",
    )(*args)
    return result if finish is not None else result[0]


def head_kernel(*refs):
    lefts, rights, outs = refs[:4], refs[4:12], refs[12:]
    depth = rights[0].shape[0]
    total = None
    for place, right in enumerate(rights):
        side = place % 2
        left = lefts[place // 2][:, side * depth : (side + 1) * depth]
        term = jnp.dot(left, right[...], preferred_element_type=F32)
        total = term if total is None else total + term
    piece = outs[0].shape[0]
    outs[0][...] = total[:piece]
    for place in range(1, 4):
        outs[place][...] = total[place * piece : (place + 1) * piece].astype(BF)


def head_products(lefts, rights):
    columns, count = lefts[0].shape
    width = rights[0].shape[1]
    depth = count // 2
    tile = 384
    piece = columns // 4
    out = pl.BlockSpec((piece, tile), lambda i: (0, i))
    mine, *sends = pl.pallas_call(
        head_kernel,
        grid=(width // tile,),
        in_specs=[pl.BlockSpec((columns, count), lambda i: (0, 0))] * 4
        + [pl.BlockSpec((depth, tile), lambda i, at=at: (at, i)) for at in (0, 1, 0, 1, 0, 1, 0, 0)],
        out_specs=[out] * 4,
        out_shape=[jax.ShapeDtypeStruct((piece, width), F32)]
        + [jax.ShapeDtypeStruct((piece, width), BF)] * 3,
        compiler_params=pltpu.CompilerParams(vmem_limit_bytes=VMEM),
        cost_estimate=pl.CostEstimate(
            flops=8 * columns * count * width, bytes_accessed=8 * 2**20, transcendentals=0
        ),
        name="head_products",
    )(*lefts, *rights)
    return mine, sends


def body(image_pool, text_pool, image_head, text_head, logit_scale, logit_bias):
    core = lax.axis_index("core")
    half = lax.axis_index("yl")
    odd = lax.axis_index("yh")
    plane = lax.axis_index("z")
    first = core == 0
    rows, width = image_pool.shape
    columns = image_head.shape[1]

    head_own = jnp.where(first, image_head, text_head).T
    head_other = jnp.where(first, text_head, image_head).T
    head_own, head_other = lax.optimization_barrier((head_own, head_other))
    pool_own = jnp.where(first, image_pool, text_pool)
    pool_other = jnp.where(first, text_pool, image_pool)
    head_up = moved(head_own, hop(dy=1))
    head_down = moved(head_other, hop(dy=-1, swap=1))
    pool_mate = moved(pool_other, hop(swap=1))
    head_mate = moved(after(head_other, pool_mate), hop(swap=1))
    pool = jnp.concatenate([pool_own, pool_mate], axis=0)
    pool_z1 = moved(pool, hop(dz=1))
    pool_z3 = moved(pool, hop(dz=-1))
    far = 1 - half
    place = jnp.stack(
        [2 * half + core, 2 * half + 1 - core, 2 * far + core, 2 * far + 1 - core]
    ).astype(jnp.int32)
    unit, emb, inverse, head = embed(
        pool_own, pool_mate, (head_own, head_mate, head_up, head_down), place
    )

    odd_block = jnp.where(first, odd, 1 - odd)
    is_odd = odd_block == 1
    score = functools.partial(
        sums, emb, scale=logit_scale, bias=logit_bias, odd=odd_block.astype(jnp.int32).reshape(1)
    )
    b0n = moved(emb, collect("same", direct=True))
    b2n = moved(emb, collect("column", direct=True))
    b0f_even = moved(emb, collect("half", parity=0, direct=True))
    b1f_odd = moved(after(emb, b0n, pool_z1, pool_z3), collect("cross", parity=0, direct=True))
    b0f_odd = moved(after(emb, b0f_even), collect("half", parity=1, direct=True))
    b1f_even = moved(b2n, collect("cross", parity=1))
    b1f_b0f = jnp.where(is_odd, b1f_odd, b0f_even)
    b3f_b2f = moved(b1f_b0f, collect("column"))
    grad = score([b0n, b2n, b1f_b0f], label=True)
    b0f_odd, b1f_even, grad = lax.optimization_barrier((b0f_odd, b1f_even, grad))
    b0f_b1f = jnp.where(is_odd, b0f_odd, b1f_even)
    b2f_b3f = moved(b0f_b1f, collect("column"))
    b1n_odd = moved(after(b1f_b0f, b1f_even), collect("cross", parity=0))
    b3n_odd = moved(b3f_b2f, collect("half", parity=1))
    grad = score([b3f_b2f, b0f_b1f], total=grad)
    b2f_b3f, b1n_odd, b3n_odd, grad = lax.optimization_barrier((b2f_b3f, b1n_odd, b3n_odd, grad))
    b1n_even = moved(b2f_b3f, collect("cross", parity=1))
    b3n_even = moved(b2f_b3f, collect("half", parity=0))
    grad = score([b2f_b3f], total=grad)
    own_z2 = moved(after(pool_z1[:rows], b2f_b3f), hop(dz=1))
    mate_z2 = moved(after(pool_z3[rows:], b2f_b3f), hop(dz=-1))
    order = []
    for ahead in range(4):
        for far_half, far_odd in ((0, 0), (0, 1), (1, 0), (1, 1)):
            shard = 2 * (half ^ far_half) + (odd ^ far_odd)
            order.append(shard * 4 + (plane + ahead) % 4)
    order = jnp.stack(order).astype(jnp.int32)
    raw_grad, *pieces = score(
        [(b1n_odd, b1n_even), (b3n_odd, b3n_even)],
        total=grad,
        finish=(unit, inverse, order),
    )
    part2 = moved(pieces[2], hop(dz=2))
    part1 = moved(pieces[1], hop(dz=1))
    part3 = moved(pieces[3], hop(dz=-1))
    grad_pool = dot_nn(raw_grad, head).astype(BF)
    pool_back = moved(grad_pool[rows:], hop(swap=1))
    grad_image = jnp.where(first, grad_pool[:rows], pool_back)
    grad_text = jnp.where(first, pool_back, grad_pool[:rows])
    part2, grad_pool = lax.optimization_barrier((part2, grad_pool))
    mine, sends = head_products(
        (pieces[0], part1, part3, part2),
        (pool, pool, pool_z1, pool_z1, pool_z3, pool_z3, own_z2, mate_z2),
    )

    def y_partner(bits):
        return lambda z, x, y, c: (z, x, y ^ bits, c)

    got = [moved(out, y_partner(bits)) for out, bits in zip(sends, (2, 1, 3))]
    for part in got:
        mine = mine + part.astype(F32)
    narrow = mine.astype(BF)
    for part in [moved(narrow, hop(dx=2)), moved(narrow, hop(dx=1)), moved(narrow, hop(dx=-1))]:
        mine = mine + part.astype(F32)
    narrow = mine.astype(BF)

    def hand_one(z, x, y, c):
        return (z, x, y, 1 - c) if c != y // 2 else (z, x, y ^ 2, c)

    def hand_two(z, x, y, c):
        return (z, x, y ^ 2, 1 - c) if c != y // 2 else None

    one = moved(narrow, hand_one)
    two = moved(narrow, hand_two)
    here = core == odd
    same = jnp.where(here, narrow, one)
    other = jnp.where(here, one, two)
    pair = jnp.stack([jnp.where(first, same, other), jnp.where(first, other, same)])
    across = moved(pair, hop(dz=2))
    ring = [pair, moved(pair, hop(dz=-1)), across, moved(pair, hop(dz=1))]
    ring = jnp.stack(ring + ring, axis=1)
    ring = lax.dynamic_slice_in_dim(ring, 4 - plane, 4, 1)
    ring = ring.reshape(2, columns, width).astype(F32)
    return (grad_image, grad_text, ring[0].T, ring[1].T)


def solution(mesh):
    fine = Mesh(mesh.devices.reshape(SIZES), AXES)
    rows = P(AXES, None)
    cols = P(None, ("yl", "core"))
    return jax.shard_map(
        body,
        mesh=fine,
        in_specs=(rows, rows, cols, cols, P(), P()),
        out_specs=(rows, rows, cols, cols),
        check_vma=False,
    )
```

```python
import functools

import jax
import jax.numpy as jnp
from jax import lax
from jax.experimental import pallas as pl
from jax.experimental.pallas import tpu as pltpu
from jax.sharding import Mesh, PartitionSpec as P

WIN = 4
COST = 10**6
VMEM = 40 * 2**20
VMEM_LARGE = 40 * 2**20
VMEM_SMALL = 24 * 2**20
AXES = ("z", "x", "yh", "yl", "core")
SIZES = (4, 4, 2, 2, 2)
BF = jnp.bfloat16
F32 = jnp.float32


def flat(z, x, y, core):
    return (((z % 4) * 4 + x % 4) * 4 + y % 4) * 2 + core


def moved(block, route):
    pairs = []
    for z in range(4):
        for x in range(4):
            for y in range(4):
                for core in range(2):
                    place = route(z, x, y, core)
                    if place is not None:
                        pairs.append((flat(z, x, y, core), flat(*place)))
    return lax.ppermute(block, AXES, pairs)


def hop(dz=0, dx=0, dy=0, swap=0):
    return lambda z, x, y, core: (z + dz, x + dx, y + dy, core ^ swap)


def collect(step, parity=None, direct=False):
    def route(z, x, y, core):
        role = core ^ 1 if direct else core
        if role:
            z, x, y = 3 - z, 3 - x, 3 - y
        column, odd, half = z * 4 + x, y // 2, y % 2
        if parity is not None and odd != parity:
            return None
        if step == "half":
            half = 1 - half
        elif step == "column":
            column = (column + 1) % 16
        elif step == "cross":
            odd, half = 1 - odd, 1 - half
        z, x, y = column // 4, column % 4, odd * 2 + half
        if role:
            z, x, y = 3 - z, 3 - x, 3 - y
        return (z, x, y, role)

    return route


def after(value, *others):
    return lax.optimization_barrier((value,) + others)[0]


def dot_nt(left, right):
    return lax.dot_general(
        left, right, (((1,), (1,)), ((), ())), preferred_element_type=F32
    )


def dot_nn(left, right):
    return jnp.dot(left, right, preferred_element_type=F32)


def embed_kernel(place, own, mate, *refs):
    parts, (unit, emb, inverse), scratch = refs[:4], refs[4:7], refs[7:]
    pool_v, head_v, unit_v, emb_v, inverse_v, sem, out_sem = scratch
    columns = parts[0].shape[0]
    rows = own.shape[0]
    copies = [
        pltpu.make_async_copy(own, pool_v.at[pl.ds(0, rows)], sem.at[4]),
        pltpu.make_async_copy(mate, pool_v.at[pl.ds(rows, rows)], sem.at[5]),
    ]
    for i, part in enumerate(parts):
        start = pl.multiple_of(place[i] * columns, 16)
        copies.append(pltpu.make_async_copy(part, head_v.at[pl.ds(start, columns)], sem.at[i]))
    for copy in copies:
        copy.start()
    for copy in copies:
        copy.wait()
    outs = []
    for i in range(2):
        half = pl.ds(i * rows, rows)
        raw = dot_nt(pool_v[half, :], head_v[...])
        norm = lax.rsqrt(jnp.sum(raw * raw, axis=1, keepdims=True) + 1e-06)
        raw = raw * norm
        emb_v[half, :] = raw.astype(BF)
        unit_v[half, :] = raw
        inverse_v[half, :] = jnp.broadcast_to(norm, (rows, 128))
        for j, (source, target) in enumerate(((emb_v, emb), (unit_v, unit), (inverse_v, inverse))):
            outs.append(
                pltpu.make_async_copy(source.at[half], target.at[half], out_sem.at[3 * i + j])
            )
            outs[-1].start()
    for out in outs:
        out.wait()


def embed(own, mate, parts, place):
    rows, width = own.shape
    shapes = [((2 * rows, width), F32), ((2 * rows, width), BF), ((2 * rows, 128), F32)]
    return pl.pallas_call(
        embed_kernel,
        in_specs=[pl.BlockSpec(memory_space=pltpu.SMEM)]
        + [pl.BlockSpec(memory_space=pltpu.HBM)] * 6,
        out_specs=[pl.BlockSpec(memory_space=pltpu.HBM)] * 3,
        out_shape=[jax.ShapeDtypeStruct(*shape) for shape in shapes],
        scratch_shapes=[
            pltpu.VMEM((2 * rows, width), BF),
            pltpu.VMEM((width, width), BF),
            pltpu.VMEM((2 * rows, width), F32),
            pltpu.VMEM((2 * rows, width), BF),
            pltpu.VMEM((2 * rows, 128), F32),
            pltpu.SemaphoreType.DMA((6,)),
            pltpu.SemaphoreType.DMA((6,)),
        ],
        compiler_params=pltpu.CompilerParams(vmem_limit_bytes=VMEM_LARGE),
        cost_estimate=pl.CostEstimate(flops=COST, bytes_accessed=2**20, transcendentals=0),
        name="embed",
    )(place, own, mate, *parts)


def sums_kernel(plan, *refs):
    names, units, label = plan
    ref = dict(zip(names, refs))
    scale, bias = ref["scale"][0], ref["bias"][0]
    step = pl.program_id(0)
    copies = {}
    for place, unit in enumerate(units):
        if isinstance(unit, tuple):
            copies[place] = [
                pltpu.make_async_copy(ref[name], ref["held"].at[place], ref["sem"].at[place])
                for name in unit
            ]
            for copy, parity in zip(copies[place], (1, 0)):
                pl.when((step == 0) & (ref["odd"][0] == parity))(copy.start)

    emb = ref["emb"][...]
    rows = emb.shape[0]
    total = ref["sum"][...] if "sum" in ref else None
    for place, unit in enumerate(units):
        if place in copies:
            pl.when(step == 0)(copies[place][0].wait)
        block = ref["held"][place] if isinstance(unit, tuple) else ref[unit][...]
        count = block.shape[0]
        score = scale * dot_nt(emb, block) + bias
        below = 1.0 + jnp.exp(-score)
        tile = pl.reciprocal(below, approx=True)
        tile = tile * (2.0 - below * tile)
        if label and place == 0:
            ids = lax.broadcasted_iota(jnp.int32, score.shape, 0) + step * rows
            jds = lax.broadcasted_iota(jnp.int32, score.shape, 1)
            shift = jnp.where(jds < count // 2, count // 2, -(count // 2))
            tile = tile - (ids == jds + shift).astype(F32)
        tile = (tile * (1.0 / (WIN * 2 * count))).astype(BF)
        term = dot_nn(tile, block)
        total = term if total is None else total + term
    if "raw" not in ref:
        ref["out"][...] = total
        return
    unit, inverse = ref["unit"][...], ref["inverse"][:, :1]
    grad = total * scale
    inner = jnp.sum(unit * grad, axis=1, keepdims=True)
    raw = (grad - unit * inner) * inverse
    ref["raw"][...] = raw.astype(BF)
    ref["turned"][...] = raw.T
    piece = ref["to0"].shape[0] // 4
    for ahead in range(4):
        parts = []
        for shard in range(4):
            start = pl.multiple_of(ref["order"][ahead * 4 + shard] * piece, 8)
            parts.append(ref["turned"][pl.ds(start, piece), :])
        ref["to%d" % ahead][...] = jnp.concatenate(parts, axis=0).astype(BF)


def sums(emb, units, scale, bias, odd, total=None, label=False, finish=None):
    count, width = emb.shape
    block = 256
    smem = pl.BlockSpec(memory_space=pltpu.SMEM)
    rows = pl.BlockSpec((block, width), lambda i: (i, 0))
    whole = pl.BlockSpec((count, width), lambda i: (0, 0))
    names, args, specs = ["scale", "bias", "odd", "emb"], [scale, bias, odd, emb], [smem] * 3 + [rows]
    plan = []
    for place, unit in enumerate(units):
        if isinstance(unit, tuple):
            pair = ("a%d" % place, "b%d" % place)
            plan.append(pair)
            names += pair
            args += unit
            specs += [pl.BlockSpec(memory_space=pl.ANY)] * 2
        else:
            plan.append("u%d" % place)
            names.append("u%d" % place)
            args.append(unit)
            specs.append(whole)
    if total is not None:
        names.append("sum")
        args.append(total)
        specs.append(rows)
    if finish is None:
        outs = [("out", (count, width), F32, rows)]
    else:
        unit, inverse, order = finish
        names += ["unit", "inverse", "order"]
        args += [unit, inverse, order]
        specs += [rows, pl.BlockSpec((block, 128), lambda i: (i, 0)), smem]
        outs = [("raw", (count, width), BF, rows)]
        part = pl.BlockSpec((width // 4, block), lambda i: (0, i))
        outs += [("to%d" % i, (width // 4, count), BF, part) for i in range(4)]
    names += [out[0] for out in outs]
    scratch = []
    if any(isinstance(unit, tuple) for unit in units):
        names += ["held", "sem"]
        scratch += [
            pltpu.VMEM((len(units), count, width), BF),
            pltpu.SemaphoreType.DMA((len(units),)),
        ]
    if finish is not None:
        names.append("turned")
        scratch.append(pltpu.VMEM((width, block), F32))
    result = pl.pallas_call(
        functools.partial(sums_kernel, (tuple(names), tuple(plan), label)),
        grid=(count // block,),
        in_specs=specs,
        out_specs=[out[3] for out in outs],
        out_shape=[jax.ShapeDtypeStruct(out[1], out[2]) for out in outs],
        scratch_shapes=scratch,
        compiler_params=pltpu.CompilerParams(vmem_limit_bytes=VMEM),
        cost_estimate=pl.CostEstimate(flops=COST, bytes_accessed=2**20, transcendentals=0),
        name="finish" if finish is not None else "sums",
    )(*args)
    return result if finish is not None else result[0]


def head_kernel(*refs):
    lefts, rights, outs = refs[:4], refs[4:9], refs[9:]
    half = rights[0].shape[0] // 2
    total = None
    for left, right in zip(lefts[:3], rights[:3]):
        term = dot_nn(left[...], right[...])
        total = term if total is None else total + term
    total = total + dot_nn(lefts[3][:, :half], rights[3][...])
    total = total + dot_nn(lefts[3][:, half:], rights[4][...])
    piece = outs[0].shape[0]
    outs[0][...] = total[:piece]
    for i in range(1, 4):
        outs[i][...] = total[i * piece : (i + 1) * piece].astype(BF)


def head_products(lefts, rights):
    columns, count = lefts[0].shape
    width = rights[0].shape[1]
    piece = columns // 4
    vmem = pl.BlockSpec(memory_space=pltpu.VMEM)
    mine, *sends = pl.pallas_call(
        head_kernel,
        in_specs=[vmem] * 9,
        out_specs=[vmem] * 4,
        out_shape=[jax.ShapeDtypeStruct((piece, width), F32)]
        + [jax.ShapeDtypeStruct((piece, width), BF)] * 3,
        compiler_params=pltpu.CompilerParams(vmem_limit_bytes=VMEM_SMALL),
        cost_estimate=pl.CostEstimate(flops=COST, bytes_accessed=2**20, transcendentals=0),
        name="head_products",
    )(*lefts, *rights)
    return mine, sends


def body(image_pool, text_pool, image_head, text_head, logit_scale, logit_bias):
    core = lax.axis_index("core")
    half = lax.axis_index("yl")
    odd = lax.axis_index("yh")
    plane = lax.axis_index("z")
    first = core == 0
    rows, width = image_pool.shape
    columns = image_head.shape[1]

    head_own = jnp.where(first, image_head, text_head).T
    head_other = jnp.where(first, text_head, image_head).T
    head_own, head_other = lax.optimization_barrier((head_own, head_other))
    pool_own = jnp.where(first, image_pool, text_pool)
    pool_other = jnp.where(first, text_pool, image_pool)
    head_up = moved(head_own, hop(dy=1))
    head_down = moved(head_other, hop(dy=-1, swap=1))
    pool_mate = moved(pool_other, hop(swap=1))
    head_mate = moved(after(head_other, pool_mate), hop(swap=1))
    pool = jnp.concatenate([pool_own, pool_mate], axis=0)
    pool_z1 = moved(pool, hop(dz=1))
    pool_z3 = moved(pool, hop(dz=-1))
    far = 1 - half
    place = jnp.stack(
        [2 * half + core, 2 * half + 1 - core, 2 * far + core, 2 * far + 1 - core]
    ).astype(jnp.int32)
    parts = (head_own, head_mate, head_up, head_down)
    unit, emb, inverse = embed(pool_own, pool_mate, parts, place)

    odd_block = jnp.where(first, odd, 1 - odd)
    is_odd = odd_block == 1
    score = functools.partial(
        sums, emb, scale=logit_scale, bias=logit_bias, odd=odd_block.astype(jnp.int32).reshape(1)
    )
    b0n = moved(emb, collect("same", direct=True))
    b2n = moved(emb, collect("column", direct=True))
    b0f_even = moved(emb, collect("half", parity=0, direct=True))
    b1f_odd = moved(after(emb, b0n, pool_z1, pool_z3), collect("cross", parity=0, direct=True))
    b0f_odd = moved(after(emb, b0f_even), collect("half", parity=1, direct=True))
    b1f_even = moved(b2n, collect("cross", parity=1))
    b1f_b0f = jnp.where(is_odd, b1f_odd, b0f_even)
    b3f_b2f = moved(b1f_b0f, collect("column"))
    grad = score([b0n, b2n, b1f_b0f], label=True)
    b0f_odd, b1f_even, grad = lax.optimization_barrier((b0f_odd, b1f_even, grad))
    b0f_b1f = jnp.where(is_odd, b0f_odd, b1f_even)
    b2f_b3f = moved(b0f_b1f, collect("column"))
    b1n_odd = moved(after(b1f_b0f, b1f_even), collect("cross", parity=0))
    b3n_odd = moved(b3f_b2f, collect("half", parity=1))
    grad = score([b3f_b2f, b0f_b1f], total=grad)
    b2f_b3f, b1n_odd, b3n_odd, grad = lax.optimization_barrier((b2f_b3f, b1n_odd, b3n_odd, grad))
    b1n_even = moved(b2f_b3f, collect("cross", parity=1))
    b3n_even = moved(b2f_b3f, collect("half", parity=0))
    grad = score([b2f_b3f], total=grad)
    own_z2 = moved(after(pool_z1[:rows], b2f_b3f), hop(dz=1))
    mate_z2 = moved(after(pool_z3[rows:], b2f_b3f), hop(dz=-1))
    order = []
    for ahead in range(4):
        for far_half, far_odd in ((0, 0), (0, 1), (1, 0), (1, 1)):
            shard = 2 * (half ^ far_half) + (odd ^ far_odd)
            order.append(shard * 4 + (plane + ahead) % 4)
    order = jnp.stack(order).astype(jnp.int32)
    raw_grad, *pieces = score(
        [(b1n_odd, b1n_even), (b3n_odd, b3n_even)],
        total=grad,
        finish=(unit, inverse, order),
    )
    part2 = moved(pieces[2], hop(dz=2))
    part1 = moved(pieces[1], hop(dz=1))
    part3 = moved(pieces[3], hop(dz=-1))
    head = jnp.zeros((width, width), BF)
    for i in range(4):
        head = lax.dynamic_update_slice(head, parts[i], (place[i] * columns, 0))
    grad_pool = dot_nn(raw_grad, head).astype(BF)
    part2, grad_pool = lax.optimization_barrier((part2, grad_pool))
    pool_back = moved(grad_pool[rows:], hop(swap=1))
    grad_image = jnp.where(first, grad_pool[:rows], pool_back)
    grad_text = jnp.where(first, pool_back, grad_pool[:rows])
    mine, sends = head_products(
        (pieces[0], part1, part3, part2),
        (pool, pool_z1, pool_z3, own_z2, mate_z2),
    )

    def y_partner(bits):
        return lambda z, x, y, c: (z, x, y ^ bits, c)

    got = [moved(out, y_partner(bits)) for out, bits in zip(sends, (2, 1, 3))]
    for part in got:
        mine = mine + part.astype(F32)
    narrow = after(mine.astype(BF), pool_back)
    for part in [moved(narrow, hop(dx=2)), moved(narrow, hop(dx=1)), moved(narrow, hop(dx=-1))]:
        mine = mine + part.astype(F32)
    narrow = mine.astype(BF)

    def hand_one(z, x, y, c):
        return (z, x, y, 1 - c) if c != y // 2 else (z, x, y ^ 2, c)

    def hand_two(z, x, y, c):
        return (z, x, y ^ 2, 1 - c) if c != y // 2 else None

    one = moved(narrow, hand_one)
    two = moved(narrow, hand_two)
    here = core == odd
    same = jnp.where(here, narrow, one)
    other = jnp.where(here, one, two)
    pair = jnp.stack([jnp.where(first, same, other), jnp.where(first, other, same)])
    pair, grad_image, grad_text = lax.optimization_barrier((pair, grad_image, grad_text))
    across = moved(pair, hop(dz=2))
    ring = [pair, moved(pair, hop(dz=-1)), across, moved(pair, hop(dz=1))]
    ring = jnp.stack(ring + ring, axis=1)
    ring = lax.dynamic_slice_in_dim(ring, 4 - plane, 4, 1)
    ring = ring.reshape(2, columns, width).astype(F32)
    return (grad_image, grad_text, ring[0].T, ring[1].T)


def solution(mesh):
    fine = Mesh(mesh.devices.reshape(SIZES), AXES)
    rows = P(AXES, None)
    cols = P(None, ("yl", "core"))
    return jax.shard_map(
        body,
        mesh=fine,
        in_specs=(rows, rows, cols, cols, P(), P()),
        out_specs=(rows, rows, cols, cols),
        check_vma=False,
    )
```

```python
import functools

import jax
import jax.numpy as jnp
from jax import lax
from jax.experimental import pallas as pl
from jax.experimental.pallas import tpu as pltpu
from jax.sharding import Mesh, PartitionSpec as P

WIN = 4
COST = 3 * 10**8
VMEM = 40 * 2**20
VMEM_LARGE = 40 * 2**20
VMEM_SMALL = 24 * 2**20
AXES = ("z", "x", "yh", "yl", "core")
SIZES = (4, 4, 2, 2, 2)
BF = jnp.bfloat16
F32 = jnp.float32


def flat(z, x, y, core):
    return (((z % 4) * 4 + x % 4) * 4 + y % 4) * 2 + core


def moved(block, route):
    pairs = []
    for z in range(4):
        for x in range(4):
            for y in range(4):
                for core in range(2):
                    place = route(z, x, y, core)
                    if place is not None:
                        pairs.append((flat(z, x, y, core), flat(*place)))
    return lax.ppermute(block, AXES, pairs)


def hop(dz=0, dx=0, dy=0, swap=0):
    return lambda z, x, y, core: (z + dz, x + dx, y + dy, core ^ swap)


def collect(step, parity=None, direct=False):
    def route(z, x, y, core):
        role = core ^ 1 if direct else core
        if role:
            z, x, y = 3 - z, 3 - x, 3 - y
        column, odd, half = z * 4 + x, y // 2, y % 2
        if parity is not None and odd != parity:
            return None
        if step == "half":
            half = 1 - half
        elif step == "column":
            column = (column + 1) % 16
        elif step == "cross":
            odd, half = 1 - odd, 1 - half
        z, x, y = column // 4, column % 4, odd * 2 + half
        if role:
            z, x, y = 3 - z, 3 - x, 3 - y
        return (z, x, y, role)

    return route


def after(value, *others):
    return lax.optimization_barrier((value,) + others)[0]


def dot_nt(left, right):
    return lax.dot_general(
        left, right, (((1,), (1,)), ((), ())), preferred_element_type=F32
    )


def dot_nn(left, right):
    return jnp.dot(left, right, preferred_element_type=F32)


def embed_kernel(place, own, mate, *refs):
    parts, (unit, emb, inverse), scratch = refs[:4], refs[4:7], refs[7:]
    pool_v, head_v, unit_v, emb_v, inverse_v, sem, out_sem = scratch
    columns = parts[0].shape[0]
    rows = own.shape[0]
    copies = [
        pltpu.make_async_copy(own, pool_v.at[pl.ds(0, rows)], sem.at[4]),
        pltpu.make_async_copy(mate, pool_v.at[pl.ds(rows, rows)], sem.at[5]),
    ]
    for i, part in enumerate(parts):
        start = pl.multiple_of(place[i] * columns, 16)
        copies.append(pltpu.make_async_copy(part, head_v.at[pl.ds(start, columns)], sem.at[i]))
    for copy in copies:
        copy.start()
    for copy in copies:
        copy.wait()
    outs = []
    for i in range(2):
        half = pl.ds(i * rows, rows)
        raw = dot_nt(pool_v[half, :], head_v[...])
        norm = lax.rsqrt(jnp.sum(raw * raw, axis=1, keepdims=True) + 1e-06)
        raw = raw * norm
        emb_v[half, :] = raw.astype(BF)
        unit_v[half, :] = raw
        inverse_v[half, :] = jnp.broadcast_to(norm, (rows, 128))
        for j, (source, target) in enumerate(((emb_v, emb), (unit_v, unit), (inverse_v, inverse))):
            outs.append(
                pltpu.make_async_copy(source.at[half], target.at[half], out_sem.at[3 * i + j])
            )
            outs[-1].start()
    for out in outs:
        out.wait()


def embed(own, mate, parts, place):
    rows, width = own.shape
    shapes = [((2 * rows, width), F32), ((2 * rows, width), BF), ((2 * rows, 128), F32)]
    return pl.pallas_call(
        embed_kernel,
        in_specs=[pl.BlockSpec(memory_space=pltpu.SMEM)]
        + [pl.BlockSpec(memory_space=pl.ANY)] * 6,
        out_specs=[pl.BlockSpec(memory_space=pl.ANY)] * 3,
        out_shape=[jax.ShapeDtypeStruct(*shape) for shape in shapes],
        scratch_shapes=[
            pltpu.VMEM((2 * rows, width), BF),
            pltpu.VMEM((width, width), BF),
            pltpu.VMEM((2 * rows, width), F32),
            pltpu.VMEM((2 * rows, width), BF),
            pltpu.VMEM((2 * rows, 128), F32),
            pltpu.SemaphoreType.DMA((6,)),
            pltpu.SemaphoreType.DMA((6,)),
        ],
        compiler_params=pltpu.CompilerParams(vmem_limit_bytes=VMEM_LARGE),
        cost_estimate=pl.CostEstimate(flops=COST, bytes_accessed=2**20, transcendentals=0),
        name="embed",
    )(place, own, mate, *parts)


def sums_kernel(plan, *refs):
    names, units, label = plan
    ref = dict(zip(names, refs))
    scale, bias = ref["scale"][0], ref["bias"][0]
    step = pl.program_id(0)
    copies = {}
    for place, unit in enumerate(units):
        if isinstance(unit, tuple):
            copies[place] = [
                pltpu.make_async_copy(ref[name], ref["held"].at[place], ref["sem"].at[place])
                for name in unit
            ]
            for copy, parity in zip(copies[place], (1, 0)):
                pl.when((step == 0) & (ref["odd"][0] == parity))(copy.start)

    emb = ref["emb"][...]
    rows = emb.shape[0]
    total = ref["sum"][...] if "sum" in ref else None
    for place, unit in enumerate(units):
        if place in copies:
            pl.when(step == 0)(copies[place][0].wait)
        block = ref["held"][place] if isinstance(unit, tuple) else ref[unit][...]
        count = block.shape[0]
        score = scale * dot_nt(emb, block) + bias
        below = 1.0 + jnp.exp(-score)
        tile = pl.reciprocal(below, approx=True)
        tile = tile * (2.0 - below * tile)
        if label and place == 0:
            ids = lax.broadcasted_iota(jnp.int32, score.shape, 0) + step * rows
            jds = lax.broadcasted_iota(jnp.int32, score.shape, 1)
            shift = jnp.where(jds < count // 2, count // 2, -(count // 2))
            tile = tile - (ids == jds + shift).astype(F32)
        tile = (tile * (1.0 / (WIN * 2 * count))).astype(BF)
        term = dot_nn(tile, block)
        total = term if total is None else total + term
    if "raw" not in ref:
        ref["out"][...] = total
        return
    unit, inverse = ref["unit"][...], ref["inverse"][:, :1]
    grad = total * scale
    inner = jnp.sum(unit * grad, axis=1, keepdims=True)
    raw = (grad - unit * inner) * inverse
    ref["raw"][...] = raw.astype(BF)
    ref["turned"][...] = raw.T
    piece = ref["to0"].shape[0] // 4
    for ahead in range(4):
        parts = []
        for shard in range(4):
            start = pl.multiple_of(ref["order"][ahead * 4 + shard] * piece, 8)
            parts.append(ref["turned"][pl.ds(start, piece), :])
        ref["to%d" % ahead][...] = jnp.concatenate(parts, axis=0).astype(BF)


def sums(emb, units, scale, bias, odd, total=None, label=False, finish=None):
    count, width = emb.shape
    block = 256
    smem = pl.BlockSpec(memory_space=pltpu.SMEM)
    rows = pl.BlockSpec((block, width), lambda i: (i, 0))
    whole = pl.BlockSpec((count, width), lambda i: (0, 0))
    names, args, specs = ["scale", "bias", "odd", "emb"], [scale, bias, odd, emb], [smem] * 3 + [rows]
    plan = []
    for place, unit in enumerate(units):
        if isinstance(unit, tuple):
            pair = ("a%d" % place, "b%d" % place)
            plan.append(pair)
            names += pair
            args += unit
            specs += [pl.BlockSpec(memory_space=pl.ANY)] * 2
        else:
            plan.append("u%d" % place)
            names.append("u%d" % place)
            args.append(unit)
            specs.append(whole)
    if total is not None:
        names.append("sum")
        args.append(total)
        specs.append(rows)
    if finish is None:
        outs = [("out", (count, width), F32, rows)]
    else:
        unit, inverse, order = finish
        names += ["unit", "inverse", "order"]
        args += [unit, inverse, order]
        specs += [rows, pl.BlockSpec((block, 128), lambda i: (i, 0)), smem]
        outs = [("raw", (count, width), BF, rows)]
        part = pl.BlockSpec((width // 4, block), lambda i: (0, i))
        outs += [("to%d" % i, (width // 4, count), BF, part) for i in range(4)]
    names += [out[0] for out in outs]
    scratch = []
    if any(isinstance(unit, tuple) for unit in units):
        names += ["held", "sem"]
        scratch += [
            pltpu.VMEM((len(units), count, width), BF),
            pltpu.SemaphoreType.DMA((len(units),)),
        ]
    if finish is not None:
        names.append("turned")
        scratch.append(pltpu.VMEM((width, block), F32))
    result = pl.pallas_call(
        functools.partial(sums_kernel, (tuple(names), tuple(plan), label)),
        grid=(count // block,),
        in_specs=specs,
        out_specs=[out[3] for out in outs],
        out_shape=[jax.ShapeDtypeStruct(out[1], out[2]) for out in outs],
        scratch_shapes=scratch,
        compiler_params=pltpu.CompilerParams(vmem_limit_bytes=VMEM),
        cost_estimate=pl.CostEstimate(flops=COST, bytes_accessed=2**20, transcendentals=0),
        name="finish" if finish is not None else "sums",
    )(*args)
    return result if finish is not None else result[0]


def head_kernel(*refs):
    lefts, rights, outs = refs[:4], refs[4:9], refs[9:]
    half = rights[0].shape[0] // 2
    total = None
    for left, right in zip(lefts[:3], rights[:3]):
        term = dot_nn(left[...], right[...])
        total = term if total is None else total + term
    total = total + dot_nn(lefts[3][:, :half], rights[3][...])
    total = total + dot_nn(lefts[3][:, half:], rights[4][...])
    piece = outs[0].shape[0]
    outs[0][...] = total[:piece]
    for i in range(1, 4):
        outs[i][...] = total[i * piece : (i + 1) * piece].astype(BF)


def head_products(lefts, rights):
    columns, count = lefts[0].shape
    width = rights[0].shape[1]
    piece = columns // 4
    vmem = pl.BlockSpec(memory_space=pltpu.VMEM)
    mine, *sends = pl.pallas_call(
        head_kernel,
        in_specs=[vmem] * 9,
        out_specs=[vmem] * 4,
        out_shape=[jax.ShapeDtypeStruct((piece, width), F32)]
        + [jax.ShapeDtypeStruct((piece, width), BF)] * 3,
        compiler_params=pltpu.CompilerParams(vmem_limit_bytes=VMEM_SMALL),
        cost_estimate=pl.CostEstimate(flops=COST, bytes_accessed=2**20, transcendentals=0),
        name="head_products",
    )(*lefts, *rights)
    return mine, sends


def body(image_pool, text_pool, image_head, text_head, logit_scale, logit_bias):
    core = lax.axis_index("core")
    half = lax.axis_index("yl")
    odd = lax.axis_index("yh")
    plane = lax.axis_index("z")
    first = core == 0
    rows, width = image_pool.shape
    columns = image_head.shape[1]

    head_own = jnp.where(first, image_head, text_head).T
    head_other = jnp.where(first, text_head, image_head).T
    head_own, head_other = lax.optimization_barrier((head_own, head_other))
    pool_own = jnp.where(first, image_pool, text_pool)
    pool_other = jnp.where(first, text_pool, image_pool)
    head_up = moved(head_own, hop(dy=1))
    head_down = moved(head_other, hop(dy=-1, swap=1))
    pool_mate = moved(pool_other, hop(swap=1))
    head_mate = moved(after(head_other, pool_mate), hop(swap=1))
    pool = jnp.concatenate([pool_own, pool_mate], axis=0)
    pool_z1 = moved(pool, hop(dz=1))
    pool_z3 = moved(pool, hop(dz=-1))
    far = 1 - half
    place = jnp.stack(
        [2 * half + core, 2 * half + 1 - core, 2 * far + core, 2 * far + 1 - core]
    ).astype(jnp.int32)
    parts = (head_own, head_mate, head_up, head_down)
    unit, emb, inverse = embed(pool_own, pool_mate, parts, place)

    odd_block = jnp.where(first, odd, 1 - odd)
    is_odd = odd_block == 1
    score = functools.partial(
        sums, emb, scale=logit_scale, bias=logit_bias, odd=odd_block.astype(jnp.int32).reshape(1)
    )
    b0n = moved(emb, collect("same", direct=True))
    b2n = moved(emb, collect("column", direct=True))
    b0f_even = moved(emb, collect("half", parity=0, direct=True))
    b1f_odd = moved(after(emb, b0n, pool_z1, pool_z3), collect("cross", parity=0, direct=True))
    b0f_odd = moved(after(emb, b0f_even), collect("half", parity=1, direct=True))
    b1f_even = moved(b2n, collect("cross", parity=1))
    b1f_b0f = jnp.where(is_odd, b1f_odd, b0f_even)
    b3f_b2f = moved(b1f_b0f, collect("column"))
    grad = score([b0n, b2n, b1f_b0f], label=True)
    b0f_odd, b1f_even, grad = lax.optimization_barrier((b0f_odd, b1f_even, grad))
    b0f_b1f = jnp.where(is_odd, b0f_odd, b1f_even)
    b2f_b3f = moved(b0f_b1f, collect("column"))
    b1n_odd = moved(after(b1f_b0f, b1f_even), collect("cross", parity=0))
    b3n_odd = moved(b3f_b2f, collect("half", parity=1))
    grad = score([b3f_b2f, b0f_b1f], total=grad)
    b2f_b3f, grad = lax.optimization_barrier((b2f_b3f, grad))
    b1n_even = moved(b2f_b3f, collect("cross", parity=1))
    b3n_even = moved(b2f_b3f, collect("half", parity=0))
    grad = score([b2f_b3f], total=grad)
    own_z2 = moved(after(pool_z1[:rows], b2f_b3f, b1n_odd, b3n_odd), hop(dz=1))
    mate_z2 = moved(after(pool_z3[rows:], b2f_b3f, b1n_odd, b3n_odd), hop(dz=-1))
    order = []
    for ahead in range(4):
        for far_half, far_odd in ((0, 0), (0, 1), (1, 0), (1, 1)):
            shard = 2 * (half ^ far_half) + (odd ^ far_odd)
            order.append(shard * 4 + (plane + ahead) % 4)
    order = jnp.stack(order).astype(jnp.int32)
    raw_grad, *pieces = score(
        [(b1n_odd, b1n_even), (b3n_odd, b3n_even)],
        total=grad,
        finish=(unit, inverse, order),
    )
    part2 = moved(pieces[2], hop(dz=2))
    part1 = moved(pieces[1], hop(dz=1))
    part3 = moved(pieces[3], hop(dz=-1))
    head = jnp.zeros((width, width), BF)
    for i in range(4):
        head = lax.dynamic_update_slice(head, parts[i], (place[i] * columns, 0))
    grad_pool = dot_nn(raw_grad, head).astype(BF)
    part2, grad_pool = lax.optimization_barrier((part2, grad_pool))
    pool_back = moved(grad_pool[rows:], hop(swap=1))
    grad_image = jnp.where(first, grad_pool[:rows], pool_back)
    grad_text = jnp.where(first, pool_back, grad_pool[:rows])
    mine, sends = head_products(
        (pieces[0], part1, part3, part2),
        (pool, pool_z1, pool_z3, own_z2, mate_z2),
    )

    def y_partner(bits):
        return lambda z, x, y, c: (z, x, y ^ bits, c)

    got = [moved(out, y_partner(bits)) for out, bits in zip(sends, (2, 1, 3))]
    for part in got:
        mine = mine + part.astype(F32)
    narrow = after(mine.astype(BF), pool_back)
    for part in [moved(narrow, hop(dx=2)), moved(narrow, hop(dx=1)), moved(narrow, hop(dx=-1))]:
        mine = mine + part.astype(F32)
    narrow = mine.astype(BF)

    def hand_one(z, x, y, c):
        return (z, x, y, 1 - c) if c != y // 2 else (z, x, y ^ 2, c)

    def hand_two(z, x, y, c):
        return (z, x, y ^ 2, 1 - c) if c != y // 2 else None

    one = moved(narrow, hand_one)
    two = moved(narrow, hand_two)
    here = core == odd
    same = jnp.where(here, narrow, one)
    other = jnp.where(here, one, two)
    pair = jnp.stack([jnp.where(first, same, other), jnp.where(first, other, same)])
    pair, grad_image, grad_text = lax.optimization_barrier((pair, grad_image, grad_text))
    across = moved(pair, hop(dz=2))
    ring = [pair, moved(pair, hop(dz=-1)), across, moved(pair, hop(dz=1))]
    ring = jnp.stack(ring + ring, axis=1)
    ring = lax.dynamic_slice_in_dim(ring, 4 - plane, 4, 1)
    ring = ring.reshape(2, columns, width).astype(F32)
    return (grad_image, grad_text, ring[0].T, ring[1].T)


def solution(mesh):
    fine = Mesh(mesh.devices.reshape(SIZES), AXES)
    rows = P(AXES, None)
    cols = P(None, ("yl", "core"))
    return jax.shard_map(
        body,
        mesh=fine,
        in_specs=(rows, rows, cols, cols, P(), P()),
        out_specs=(rows, rows, cols, cols),
        check_vma=False,
    )
```

```python
import functools

import jax
import jax.numpy as jnp
from jax import lax
from jax.experimental import pallas as pl
from jax.experimental.pallas import tpu as pltpu
from jax.sharding import Mesh, PartitionSpec as P

WIN = 4
COST = 3 * 10**8
VMEM = 40 * 2**20
VMEM_LARGE = 40 * 2**20
VMEM_SMALL = 24 * 2**20
AXES = ("z", "x", "yh", "yl", "core")
SIZES = (4, 4, 2, 2, 2)
BF = jnp.bfloat16
F32 = jnp.float32


def flat(z, x, y, core):
    return (((z % 4) * 4 + x % 4) * 4 + y % 4) * 2 + core


def moved(block, route):
    pairs = []
    for z in range(4):
        for x in range(4):
            for y in range(4):
                for core in range(2):
                    place = route(z, x, y, core)
                    if place is not None:
                        pairs.append((flat(z, x, y, core), flat(*place)))
    return lax.ppermute(block, AXES, pairs)


def hop(dz=0, dx=0, dy=0, swap=0):
    return lambda z, x, y, core: (z + dz, x + dx, y + dy, core ^ swap)


def collect(step, parity=None, direct=False):
    def route(z, x, y, core):
        role = core ^ 1 if direct else core
        if role:
            z, x, y = 3 - z, 3 - x, 3 - y
        column, odd, half = z * 4 + x, y // 2, y % 2
        if parity is not None and odd != parity:
            return None
        if step == "half":
            half = 1 - half
        elif step == "column":
            column = (column + 1) % 16
        elif step == "cross":
            odd, half = 1 - odd, 1 - half
        z, x, y = column // 4, column % 4, odd * 2 + half
        if role:
            z, x, y = 3 - z, 3 - x, 3 - y
        return (z, x, y, role)

    return route


def after(value, *others):
    return lax.optimization_barrier((value,) + others)[0]


def dot_nt(left, right):
    return lax.dot_general(
        left, right, (((1,), (1,)), ((), ())), preferred_element_type=F32
    )


def dot_nn(left, right):
    return jnp.dot(left, right, preferred_element_type=F32)


def embed_kernel(place, own, mate, *refs):
    parts, (unit, emb, inverse), scratch = refs[:4], refs[4:7], refs[7:]
    pool_v, head_v, unit_v, emb_v, inverse_v, sem, out_sem = scratch
    columns = parts[0].shape[0]
    rows = own.shape[0]
    copies = [
        pltpu.make_async_copy(own, pool_v.at[pl.ds(0, rows)], sem.at[4]),
        pltpu.make_async_copy(mate, pool_v.at[pl.ds(rows, rows)], sem.at[5]),
    ]
    for i, part in enumerate(parts):
        start = pl.multiple_of(place[i] * columns, 16)
        copies.append(pltpu.make_async_copy(part, head_v.at[pl.ds(start, columns)], sem.at[i]))
    for copy in copies:
        copy.start()
    for copy in copies:
        copy.wait()
    outs = []
    for i in range(2):
        half = pl.ds(i * rows, rows)
        raw = dot_nt(pool_v[half, :], head_v[...])
        norm = lax.rsqrt(jnp.sum(raw * raw, axis=1, keepdims=True) + 1e-06)
        raw = raw * norm
        emb_v[half, :] = raw.astype(BF)
        unit_v[half, :] = raw
        inverse_v[half, :] = jnp.broadcast_to(norm, (rows, 128))
        for j, (source, target) in enumerate(((emb_v, emb), (unit_v, unit), (inverse_v, inverse))):
            outs.append(
                pltpu.make_async_copy(source.at[half], target.at[half], out_sem.at[3 * i + j])
            )
            outs[-1].start()
    for out in outs:
        out.wait()


def embed(own, mate, parts, place):
    rows, width = own.shape
    shapes = [((2 * rows, width), F32), ((2 * rows, width), BF), ((2 * rows, 128), F32)]
    return pl.pallas_call(
        embed_kernel,
        in_specs=[pl.BlockSpec(memory_space=pltpu.SMEM)]
        + [pl.BlockSpec(memory_space=pl.ANY)] * 6,
        out_specs=[pl.BlockSpec(memory_space=pl.ANY)] * 3,
        out_shape=[jax.ShapeDtypeStruct(*shape) for shape in shapes],
        scratch_shapes=[
            pltpu.VMEM((2 * rows, width), BF),
            pltpu.VMEM((width, width), BF),
            pltpu.VMEM((2 * rows, width), F32),
            pltpu.VMEM((2 * rows, width), BF),
            pltpu.VMEM((2 * rows, 128), F32),
            pltpu.SemaphoreType.DMA((6,)),
            pltpu.SemaphoreType.DMA((6,)),
        ],
        compiler_params=pltpu.CompilerParams(vmem_limit_bytes=VMEM_LARGE),
        cost_estimate=pl.CostEstimate(flops=COST, bytes_accessed=2**20, transcendentals=0),
        name="embed",
    )(place, own, mate, *parts)


def sums_kernel(plan, *refs):
    names, units, label = plan
    ref = dict(zip(names, refs))
    scale, bias = ref["scale"][0], ref["bias"][0]
    step = pl.program_id(0)
    copies = {}
    for place, unit in enumerate(units):
        if isinstance(unit, tuple):
            copies[place] = [
                pltpu.make_async_copy(ref[name], ref["held"].at[place], ref["sem"].at[place])
                for name in unit
            ]
            for copy, parity in zip(copies[place], (1, 0)):
                pl.when((step == 0) & (ref["odd"][0] == parity))(copy.start)

    emb = ref["emb"][...]
    rows = emb.shape[0]
    total = ref["sum"][...] if "sum" in ref else None
    for place, unit in enumerate(units):
        if place in copies:
            pl.when(step == 0)(copies[place][0].wait)
        block = ref["held"][place] if isinstance(unit, tuple) else ref[unit][...]
        count = block.shape[0]
        score = scale * dot_nt(emb, block) + bias
        below = 1.0 + jnp.exp(-score)
        tile = pl.reciprocal(below, approx=True)
        tile = tile * (2.0 - below * tile)
        if label and place == 0:
            ids = lax.broadcasted_iota(jnp.int32, score.shape, 0) + step * rows
            jds = lax.broadcasted_iota(jnp.int32, score.shape, 1)
            shift = jnp.where(jds < count // 2, count // 2, -(count // 2))
            tile = tile - (ids == jds + shift).astype(F32)
        tile = (tile * (1.0 / (WIN * 2 * count))).astype(BF)
        term = dot_nn(tile, block)
        total = term if total is None else total + term
    if "raw" not in ref:
        ref["out"][...] = total
        return
    unit, inverse = ref["unit"][...], ref["inverse"][:, :1]
    grad = total * scale
    inner = jnp.sum(unit * grad, axis=1, keepdims=True)
    raw = (grad - unit * inner) * inverse
    ref["raw"][...] = raw.astype(BF)
    ref["turned"][...] = raw.T
    piece = ref["to0"].shape[0] // 4
    for ahead in range(4):
        parts = []
        for shard in range(4):
            start = pl.multiple_of(ref["order"][ahead * 4 + shard] * piece, 8)
            parts.append(ref["turned"][pl.ds(start, piece), :])
        ref["to%d" % ahead][...] = jnp.concatenate(parts, axis=0).astype(BF)


def sums(emb, units, scale, bias, odd, total=None, label=False, finish=None):
    count, width = emb.shape
    block = 256
    smem = pl.BlockSpec(memory_space=pltpu.SMEM)
    rows = pl.BlockSpec((block, width), lambda i: (i, 0))
    whole = pl.BlockSpec((count, width), lambda i: (0, 0))
    names, args, specs = ["scale", "bias", "odd", "emb"], [scale, bias, odd, emb], [smem] * 3 + [rows]
    plan = []
    for place, unit in enumerate(units):
        if isinstance(unit, tuple):
            pair = ("a%d" % place, "b%d" % place)
            plan.append(pair)
            names += pair
            args += unit
            specs += [pl.BlockSpec(memory_space=pl.ANY)] * 2
        else:
            plan.append("u%d" % place)
            names.append("u%d" % place)
            args.append(unit)
            specs.append(whole)
    if total is not None:
        names.append("sum")
        args.append(total)
        specs.append(rows)
    if finish is None:
        outs = [("out", (count, width), F32, rows)]
    else:
        unit, inverse, order = finish
        names += ["unit", "inverse", "order"]
        args += [unit, inverse, order]
        specs += [rows, pl.BlockSpec((block, 128), lambda i: (i, 0)), smem]
        outs = [("raw", (count, width), BF, rows)]
        part = pl.BlockSpec((width // 4, block), lambda i: (0, i))
        outs += [("to%d" % i, (width // 4, count), BF, part) for i in range(4)]
    names += [out[0] for out in outs]
    scratch = []
    if any(isinstance(unit, tuple) for unit in units):
        names += ["held", "sem"]
        scratch += [
            pltpu.VMEM((len(units), count, width), BF),
            pltpu.SemaphoreType.DMA((len(units),)),
        ]
    if finish is not None:
        names.append("turned")
        scratch.append(pltpu.VMEM((width, block), F32))
    result = pl.pallas_call(
        functools.partial(sums_kernel, (tuple(names), tuple(plan), label)),
        grid=(count // block,),
        in_specs=specs,
        out_specs=[out[3] for out in outs],
        out_shape=[jax.ShapeDtypeStruct(out[1], out[2]) for out in outs],
        scratch_shapes=scratch,
        compiler_params=pltpu.CompilerParams(vmem_limit_bytes=VMEM),
        cost_estimate=pl.CostEstimate(flops=COST, bytes_accessed=2**20, transcendentals=0),
        name="finish" if finish is not None else "sums",
    )(*args)
    return result if finish is not None else result[0]


def head_kernel(*refs):
    lefts, rights, outs = refs[:4], refs[4:9], refs[9:]
    half = rights[0].shape[0] // 2
    total = None
    for left, right in zip(lefts[:3], rights[:3]):
        term = dot_nn(left[...], right[...])
        total = term if total is None else total + term
    total = total + dot_nn(lefts[3][:, :half], rights[3][...])
    total = total + dot_nn(lefts[3][:, half:], rights[4][...])
    piece = outs[0].shape[0]
    outs[0][...] = total[:piece]
    for i in range(1, 4):
        outs[i][...] = total[i * piece : (i + 1) * piece].astype(BF)


def head_products(lefts, rights):
    columns, count = lefts[0].shape
    width = rights[0].shape[1]
    piece = columns // 4
    vmem = pl.BlockSpec(memory_space=pltpu.VMEM)
    mine, *sends = pl.pallas_call(
        head_kernel,
        in_specs=[vmem] * 9,
        out_specs=[vmem] * 4,
        out_shape=[jax.ShapeDtypeStruct((piece, width), F32)]
        + [jax.ShapeDtypeStruct((piece, width), BF)] * 3,
        compiler_params=pltpu.CompilerParams(vmem_limit_bytes=VMEM_SMALL),
        cost_estimate=pl.CostEstimate(flops=COST, bytes_accessed=2**20, transcendentals=0),
        name="head_products",
    )(*lefts, *rights)
    return mine, sends


def body(image_pool, text_pool, image_head, text_head, logit_scale, logit_bias):
    core = lax.axis_index("core")
    half = lax.axis_index("yl")
    odd = lax.axis_index("yh")
    plane = lax.axis_index("z")
    first = core == 0
    rows, width = image_pool.shape
    columns = image_head.shape[1]

    head_own = jnp.where(first, image_head, text_head).T
    head_other = jnp.where(first, text_head, image_head).T
    head_own, head_other = lax.optimization_barrier((head_own, head_other))
    pool_own = jnp.where(first, image_pool, text_pool)
    pool_other = jnp.where(first, text_pool, image_pool)
    head_up = moved(head_own, hop(dy=1))
    head_down = moved(head_other, hop(dy=-1, swap=1))
    pool_mate = moved(pool_other, hop(swap=1))
    head_mate = moved(after(head_other, pool_mate), hop(swap=1))
    pool = jnp.concatenate([pool_own, pool_mate], axis=0)
    pool_z1 = moved(pool, hop(dz=1))
    pool_z3 = moved(pool, hop(dz=-1))
    far = 1 - half
    place = jnp.stack(
        [2 * half + core, 2 * half + 1 - core, 2 * far + core, 2 * far + 1 - core]
    ).astype(jnp.int32)
    parts = (head_own, head_mate, head_up, head_down)
    unit, emb, inverse = embed(pool_own, pool_mate, parts, place)

    odd_block = jnp.where(first, odd, 1 - odd)
    is_odd = odd_block == 1
    score = functools.partial(
        sums, emb, scale=logit_scale, bias=logit_bias, odd=odd_block.astype(jnp.int32).reshape(1)
    )
    b0n = moved(emb, collect("same", direct=True))
    b2n = moved(emb, collect("column", direct=True))
    b0f_even = moved(emb, collect("half", parity=0, direct=True))
    b1f_odd = moved(after(emb, b0n, pool_z1, pool_z3), collect("cross", parity=0, direct=True))
    b0f_odd = moved(after(emb, b0f_even), collect("half", parity=1, direct=True))
    b1f_even = moved(b2n, collect("cross", parity=1))
    b1f_b0f = jnp.where(is_odd, b1f_odd, b0f_even)
    b3f_b2f = moved(b1f_b0f, collect("column"))
    grad = score([b0n, b2n, b1f_b0f], label=True)
    b0f_odd, b1f_even, grad = lax.optimization_barrier((b0f_odd, b1f_even, grad))
    b0f_b1f = jnp.where(is_odd, b0f_odd, b1f_even)
    b2f_b3f = moved(b0f_b1f, collect("column"))
    b1n_odd = moved(after(b1f_b0f, b1f_even), collect("cross", parity=0))
    b3n_odd = moved(b3f_b2f, collect("half", parity=1))
    grad = score([b3f_b2f, b0f_b1f], total=grad)
    b2f_b3f, grad = lax.optimization_barrier((b2f_b3f, grad))
    b1n_even = moved(b2f_b3f, collect("cross", parity=1))
    b3n_even = moved(b2f_b3f, collect("half", parity=0))
    grad = score([b2f_b3f], total=grad)
    own_z2 = moved(after(pool_z1[:rows], b2f_b3f, b1n_odd, b3n_odd), hop(dz=1))
    mate_z2 = moved(after(pool_z3[rows:], b2f_b3f, b1n_odd, b3n_odd), hop(dz=-1))
    order = []
    for ahead in range(4):
        for far_half, far_odd in ((0, 0), (0, 1), (1, 0), (1, 1)):
            shard = 2 * (half ^ far_half) + (odd ^ far_odd)
            order.append(shard * 4 + (plane + ahead) % 4)
    order = jnp.stack(order).astype(jnp.int32)
    raw_grad, *pieces = score(
        [(b1n_odd, b1n_even), (b3n_odd, b3n_even)],
        total=grad,
        finish=(unit, inverse, order),
    )
    part2 = moved(pieces[2], hop(dz=2))
    part1 = moved(pieces[1], hop(dz=1))
    part3 = moved(pieces[3], hop(dz=-1))
    head = jnp.zeros((width, width), BF)
    for i in range(4):
        head = lax.dynamic_update_slice(head, parts[i], (place[i] * columns, 0))
    grad_pool = dot_nn(raw_grad, head).astype(BF)
    part2, grad_pool = lax.optimization_barrier((part2, grad_pool))
    pool_back = moved(grad_pool[rows:], hop(swap=1))
    grad_image = jnp.where(first, grad_pool[:rows], pool_back)
    grad_text = jnp.where(first, pool_back, grad_pool[:rows])
    mine, sends = head_products(
        (pieces[0], part1, part3, part2),
        (pool, pool_z1, pool_z3, own_z2, mate_z2),
    )

    def y_partner(bits):
        return lambda z, x, y, c: (z, x, y ^ bits, c)

    got = [moved(out, y_partner(bits)) for out, bits in zip(sends, (2, 1, 3))]
    for part in got:
        mine = mine + part.astype(F32)
    narrow = after(mine.astype(BF), pool_back)
    for part in [moved(narrow, hop(dx=2)), moved(narrow, hop(dx=1)), moved(narrow, hop(dx=-1))]:
        mine = mine + part.astype(F32)
    narrow = mine.astype(BF)

    def hand_one(z, x, y, c):
        return (z, x, y, 1 - c) if c != y // 2 else (z, x, y ^ 2, c)

    def hand_two(z, x, y, c):
        return (z, x, y ^ 2, 1 - c) if c != y // 2 else None

    one = moved(narrow, hand_one)
    two = moved(narrow, hand_two)
    here = core == odd
    same = jnp.where(here, narrow, one)
    other = jnp.where(here, one, two)
    pair = jnp.stack([jnp.where(first, same, other), jnp.where(first, other, same)])
    pair, grad_image, grad_text = lax.optimization_barrier((pair, grad_image, grad_text))
    below, above = moved(pair, hop(dz=1)), moved(pair, hop(dz=-1))
    across = jnp.stack([moved(below[0], hop(dz=1)), moved(above[1], hop(dz=-1))])
    ring = [pair, above, across, below]
    ring = jnp.stack(ring + ring, axis=1)
    ring = lax.dynamic_slice_in_dim(ring, 4 - plane, 4, 1)
    ring = ring.reshape(2, columns, width).astype(F32)
    return (grad_image, grad_text, ring[0].T, ring[1].T)


def solution(mesh):
    fine = Mesh(mesh.devices.reshape(SIZES), AXES)
    rows = P(AXES, None)
    cols = P(None, ("yl", "core"))
    return jax.shard_map(
        body,
        mesh=fine,
        in_specs=(rows, rows, cols, cols, P(), P()),
        out_specs=(rows, rows, cols, cols),
        check_vma=False,
    )
```

```python
import functools

import jax
import jax.numpy as jnp
from jax import lax
from jax.experimental import pallas as pl
from jax.experimental.pallas import tpu as pltpu
from jax.sharding import Mesh, PartitionSpec as P

WIN = 4
COST = 3 * 10**8
VMEM = 40 * 2**20
VMEM_LARGE = 40 * 2**20
VMEM_SMALL = 24 * 2**20
AXES = ("z", "x", "yh", "yl", "core")
SIZES = (4, 4, 2, 2, 2)
BF = jnp.bfloat16
F32 = jnp.float32


def flat(z, x, y, core):
    return (((z % 4) * 4 + x % 4) * 4 + y % 4) * 2 + core


def moved(block, route):
    pairs = []
    for z in range(4):
        for x in range(4):
            for y in range(4):
                for core in range(2):
                    place = route(z, x, y, core)
                    if place is not None:
                        pairs.append((flat(z, x, y, core), flat(*place)))
    return lax.ppermute(block, AXES, pairs)


def hop(dz=0, dx=0, dy=0, swap=0):
    return lambda z, x, y, core: (z + dz, x + dx, y + dy, core ^ swap)


def collect(step, parity=None, direct=False):
    def route(z, x, y, core):
        role = core ^ 1 if direct else core
        if role:
            z, x, y = 3 - z, 3 - x, 3 - y
        column, odd, half = z * 4 + x, y // 2, y % 2
        if parity is not None and odd != parity:
            return None
        if step == "half":
            half = 1 - half
        elif step == "column":
            column = (column + 1) % 16
        elif step == "cross":
            odd, half = 1 - odd, 1 - half
        z, x, y = column // 4, column % 4, odd * 2 + half
        if role:
            z, x, y = 3 - z, 3 - x, 3 - y
        return (z, x, y, role)

    return route


def after(value, *others):
    return lax.optimization_barrier((value,) + others)[0]


def dot_nt(left, right):
    return lax.dot_general(
        left, right, (((1,), (1,)), ((), ())), preferred_element_type=F32
    )


def dot_nn(left, right):
    return jnp.dot(left, right, preferred_element_type=F32)


def embed_kernel(place, own, mate, *refs):
    parts, (unit, emb, inverse), scratch = refs[:4], refs[4:7], refs[7:]
    pool_v, head_v, unit_v, emb_v, inverse_v, sem, out_sem = scratch
    columns = parts[0].shape[0]
    rows = own.shape[0]
    copies = [
        pltpu.make_async_copy(own, pool_v.at[pl.ds(0, rows)], sem.at[4]),
        pltpu.make_async_copy(mate, pool_v.at[pl.ds(rows, rows)], sem.at[5]),
    ]
    for i, part in enumerate(parts):
        start = pl.multiple_of(place[i] * columns, 16)
        copies.append(pltpu.make_async_copy(part, head_v.at[pl.ds(start, columns)], sem.at[i]))
    for copy in copies:
        copy.start()
    for copy in copies:
        copy.wait()
    outs = []
    for i in range(2):
        half = pl.ds(i * rows, rows)
        raw = dot_nt(pool_v[half, :], head_v[...])
        norm = lax.rsqrt(jnp.sum(raw * raw, axis=1, keepdims=True) + 1e-06)
        raw = raw * norm
        emb_v[half, :] = raw.astype(BF)
        unit_v[half, :] = raw
        inverse_v[half, :] = jnp.broadcast_to(norm, (rows, 128))
        for j, (source, target) in enumerate(((emb_v, emb), (unit_v, unit), (inverse_v, inverse))):
            outs.append(
                pltpu.make_async_copy(source.at[half], target.at[half], out_sem.at[3 * i + j])
            )
            outs[-1].start()
    for out in outs:
        out.wait()


def embed(own, mate, parts, place):
    rows, width = own.shape
    shapes = [((2 * rows, width), F32), ((2 * rows, width), BF), ((2 * rows, 128), F32)]
    return pl.pallas_call(
        embed_kernel,
        in_specs=[pl.BlockSpec(memory_space=pltpu.SMEM)]
        + [pl.BlockSpec(memory_space=pl.ANY)] * 6,
        out_specs=[pl.BlockSpec(memory_space=pl.ANY)] * 3,
        out_shape=[jax.ShapeDtypeStruct(*shape) for shape in shapes],
        scratch_shapes=[
            pltpu.VMEM((2 * rows, width), BF),
            pltpu.VMEM((width, width), BF),
            pltpu.VMEM((2 * rows, width), F32),
            pltpu.VMEM((2 * rows, width), BF),
            pltpu.VMEM((2 * rows, 128), F32),
            pltpu.SemaphoreType.DMA((6,)),
            pltpu.SemaphoreType.DMA((6,)),
        ],
        compiler_params=pltpu.CompilerParams(vmem_limit_bytes=VMEM_LARGE),
        cost_estimate=pl.CostEstimate(flops=COST, bytes_accessed=2**20, transcendentals=0),
        name="embed",
    )(place, own, mate, *parts)


def sums_kernel(plan, *refs):
    names, units, label = plan
    ref = dict(zip(names, refs))
    scale, bias = ref["scale"][0], ref["bias"][0]
    step = pl.program_id(0)
    copies = {}
    for place, unit in enumerate(units):
        if isinstance(unit, tuple):
            copies[place] = [
                pltpu.make_async_copy(ref[name], ref["held"].at[place], ref["sem"].at[place])
                for name in unit
            ]
            for copy, parity in zip(copies[place], (1, 0)):
                pl.when((step == 0) & (ref["odd"][0] == parity))(copy.start)

    emb = ref["emb"][...]
    rows = emb.shape[0]
    total = ref["sum"][...] if "sum" in ref else None
    for place, unit in enumerate(units):
        if place in copies:
            pl.when(step == 0)(copies[place][0].wait)
        block = ref["held"][place] if isinstance(unit, tuple) else ref[unit][...]
        count = block.shape[0]
        score = scale * dot_nt(emb, block) + bias
        below = 1.0 + jnp.exp(-score)
        tile = pl.reciprocal(below, approx=True)
        tile = tile * (2.0 - below * tile)
        if label and place == 0:
            ids = lax.broadcasted_iota(jnp.int32, score.shape, 0) + step * rows
            jds = lax.broadcasted_iota(jnp.int32, score.shape, 1)
            shift = jnp.where(jds < count // 2, count // 2, -(count // 2))
            tile = tile - (ids == jds + shift).astype(F32)
        tile = (tile * (1.0 / (WIN * 2 * count))).astype(BF)
        term = dot_nn(tile, block)
        total = term if total is None else total + term
    if "raw" not in ref:
        ref["out"][...] = total
        return
    unit, inverse = ref["unit"][...], ref["inverse"][:, :1]
    grad = total * scale
    inner = jnp.sum(unit * grad, axis=1, keepdims=True)
    raw = (grad - unit * inner) * inverse
    ref["raw"][...] = raw.astype(BF)
    ref["turned"][...] = raw.T
    piece = ref["to0"].shape[0] // 4
    for ahead in range(4):
        parts = []
        for shard in range(4):
            start = pl.multiple_of(ref["order"][ahead * 4 + shard] * piece, 8)
            parts.append(ref["turned"][pl.ds(start, piece), :])
        ref["to%d" % ahead][...] = jnp.concatenate(parts, axis=0).astype(BF)


def sums(emb, units, scale, bias, odd, total=None, label=False, finish=None):
    count, width = emb.shape
    block = 512
    smem = pl.BlockSpec(memory_space=pltpu.SMEM)
    rows = pl.BlockSpec((block, width), lambda i: (i, 0))
    whole = pl.BlockSpec((count, width), lambda i: (0, 0))
    names, args, specs = ["scale", "bias", "odd", "emb"], [scale, bias, odd, emb], [smem] * 3 + [rows]
    plan = []
    for place, unit in enumerate(units):
        if isinstance(unit, tuple):
            pair = ("a%d" % place, "b%d" % place)
            plan.append(pair)
            names += pair
            args += unit
            specs += [pl.BlockSpec(memory_space=pl.ANY)] * 2
        else:
            plan.append("u%d" % place)
            names.append("u%d" % place)
            args.append(unit)
            specs.append(whole)
    if total is not None:
        names.append("sum")
        args.append(total)
        specs.append(rows)
    if finish is None:
        outs = [("out", (count, width), F32, rows)]
    else:
        unit, inverse, order = finish
        names += ["unit", "inverse", "order"]
        args += [unit, inverse, order]
        specs += [rows, pl.BlockSpec((block, 128), lambda i: (i, 0)), smem]
        outs = [("raw", (count, width), BF, rows)]
        part = pl.BlockSpec((width // 4, block), lambda i: (0, i))
        outs += [("to%d" % i, (width // 4, count), BF, part) for i in range(4)]
    names += [out[0] for out in outs]
    scratch = []
    if any(isinstance(unit, tuple) for unit in units):
        names += ["held", "sem"]
        scratch += [
            pltpu.VMEM((len(units), count, width), BF),
            pltpu.SemaphoreType.DMA((len(units),)),
        ]
    if finish is not None:
        names.append("turned")
        scratch.append(pltpu.VMEM((width, block), F32))
    result = pl.pallas_call(
        functools.partial(sums_kernel, (tuple(names), tuple(plan), label)),
        grid=(count // block,),
        in_specs=specs,
        out_specs=[out[3] for out in outs],
        out_shape=[jax.ShapeDtypeStruct(out[1], out[2]) for out in outs],
        scratch_shapes=scratch,
        compiler_params=pltpu.CompilerParams(vmem_limit_bytes=VMEM),
        cost_estimate=pl.CostEstimate(flops=COST, bytes_accessed=2**20, transcendentals=0),
        name="finish" if finish is not None else "sums",
    )(*args)
    return result if finish is not None else result[0]


def head_kernel(*refs):
    lefts, rights, outs = refs[:4], refs[4:9], refs[9:]
    half = rights[0].shape[0] // 2
    total = None
    for left, right in zip(lefts[:3], rights[:3]):
        term = dot_nn(left[...], right[...])
        total = term if total is None else total + term
    total = total + dot_nn(lefts[3][:, :half], rights[3][...])
    total = total + dot_nn(lefts[3][:, half:], rights[4][...])
    piece = outs[0].shape[0]
    outs[0][...] = total[:piece]
    for i in range(1, 4):
        outs[i][...] = total[i * piece : (i + 1) * piece].astype(BF)


def head_products(lefts, rights):
    columns, count = lefts[0].shape
    width = rights[0].shape[1]
    piece = columns // 4
    vmem = pl.BlockSpec(memory_space=pltpu.VMEM)
    mine, *sends = pl.pallas_call(
        head_kernel,
        in_specs=[vmem] * 9,
        out_specs=[vmem] * 4,
        out_shape=[jax.ShapeDtypeStruct((piece, width), F32)]
        + [jax.ShapeDtypeStruct((piece, width), BF)] * 3,
        compiler_params=pltpu.CompilerParams(vmem_limit_bytes=VMEM_SMALL),
        cost_estimate=pl.CostEstimate(flops=COST, bytes_accessed=2**20, transcendentals=0),
        name="head_products",
    )(*lefts, *rights)
    return mine, sends


def body(image_pool, text_pool, image_head, text_head, logit_scale, logit_bias):
    core = lax.axis_index("core")
    half = lax.axis_index("yl")
    odd = lax.axis_index("yh")
    plane = lax.axis_index("z")
    first = core == 0
    rows, width = image_pool.shape
    columns = image_head.shape[1]

    head_own = jnp.where(first, image_head, text_head).T
    head_other = jnp.where(first, text_head, image_head).T
    head_own, head_other = lax.optimization_barrier((head_own, head_other))
    pool_own = jnp.where(first, image_pool, text_pool)
    pool_other = jnp.where(first, text_pool, image_pool)
    head_up = moved(head_own, hop(dy=1))
    head_down = moved(head_other, hop(dy=-1, swap=1))
    pool_mate = moved(pool_other, hop(swap=1))
    head_mate = moved(after(head_other, pool_mate), hop(swap=1))
    pool = jnp.concatenate([pool_own, pool_mate], axis=0)
    pool_z1 = moved(pool, hop(dz=1))
    pool_z3 = moved(pool, hop(dz=-1))
    far = 1 - half
    place = jnp.stack(
        [2 * half + core, 2 * half + 1 - core, 2 * far + core, 2 * far + 1 - core]
    ).astype(jnp.int32)
    parts = (head_own, head_mate, head_up, head_down)
    unit, emb, inverse = embed(pool_own, pool_mate, parts, place)

    odd_block = jnp.where(first, odd, 1 - odd)
    is_odd = odd_block == 1
    score = functools.partial(
        sums, emb, scale=logit_scale, bias=logit_bias, odd=odd_block.astype(jnp.int32).reshape(1)
    )
    b0n = moved(emb, collect("same", direct=True))
    b2n = moved(emb, collect("column", direct=True))
    b0f_even = moved(emb, collect("half", parity=0, direct=True))
    b1f_odd = moved(after(emb, b0n, pool_z1, pool_z3), collect("cross", parity=0, direct=True))
    b0f_odd = moved(after(emb, b0f_even), collect("half", parity=1, direct=True))
    b1f_even = moved(b2n, collect("cross", parity=1))
    b1f_b0f = jnp.where(is_odd, b1f_odd, b0f_even)
    b3f_b2f = moved(b1f_b0f, collect("column"))
    grad = score([b0n, b2n, b1f_b0f], label=True)
    b0f_odd, b1f_even, grad = lax.optimization_barrier((b0f_odd, b1f_even, grad))
    b0f_b1f = jnp.where(is_odd, b0f_odd, b1f_even)
    b2f_b3f = moved(b0f_b1f, collect("column"))
    b1n_odd = moved(after(b1f_b0f, b1f_even), collect("cross", parity=0))
    b3n_odd = moved(b3f_b2f, collect("half", parity=1))
    grad = score([b3f_b2f, b0f_b1f], total=grad)
    b2f_b3f, grad = lax.optimization_barrier((b2f_b3f, grad))
    b1n_even = moved(b2f_b3f, collect("cross", parity=1))
    b3n_even = moved(b2f_b3f, collect("half", parity=0))
    grad = score([b2f_b3f], total=grad)
    own_z2 = moved(after(pool_z1[:rows], b2f_b3f, b1n_odd, b3n_odd), hop(dz=1))
    mate_z2 = moved(after(pool_z3[rows:], b2f_b3f, b1n_odd, b3n_odd), hop(dz=-1))
    order = []
    for ahead in range(4):
        for far_half, far_odd in ((0, 0), (0, 1), (1, 0), (1, 1)):
            shard = 2 * (half ^ far_half) + (odd ^ far_odd)
            order.append(shard * 4 + (plane + ahead) % 4)
    order = jnp.stack(order).astype(jnp.int32)
    raw_grad, *pieces = score(
        [(b1n_odd, b1n_even), (b3n_odd, b3n_even)],
        total=grad,
        finish=(unit, inverse, order),
    )
    part2 = moved(pieces[2], hop(dz=2))
    part1 = moved(pieces[1], hop(dz=1))
    part3 = moved(pieces[3], hop(dz=-1))
    head = jnp.zeros((width, width), BF)
    for i in range(4):
        head = lax.dynamic_update_slice(head, parts[i], (place[i] * columns, 0))
    grad_pool = dot_nn(raw_grad, head).astype(BF)
    part2, grad_pool = lax.optimization_barrier((part2, grad_pool))
    pool_back = moved(grad_pool[rows:], hop(swap=1))
    grad_image = jnp.where(first, grad_pool[:rows], pool_back)
    grad_text = jnp.where(first, pool_back, grad_pool[:rows])
    mine, sends = head_products(
        (pieces[0], part1, part3, part2),
        (pool, pool_z1, pool_z3, own_z2, mate_z2),
    )

    def y_partner(bits):
        return lambda z, x, y, c: (z, x, y ^ bits, c)

    got = [moved(out, y_partner(bits)) for out, bits in zip(sends, (2, 1, 3))]
    for part in got:
        mine = mine + part.astype(F32)
    narrow = after(mine.astype(BF), pool_back)
    for part in [moved(narrow, hop(dx=2)), moved(narrow, hop(dx=1)), moved(narrow, hop(dx=-1))]:
        mine = mine + part.astype(F32)
    narrow = mine.astype(BF)

    def hand_one(z, x, y, c):
        return (z, x, y, 1 - c) if c != y // 2 else (z, x, y ^ 2, c)

    def hand_two(z, x, y, c):
        return (z, x, y ^ 2, 1 - c) if c != y // 2 else None

    one = moved(narrow, hand_one)
    two = moved(narrow, hand_two)
    here = core == odd
    same = jnp.where(here, narrow, one)
    other = jnp.where(here, one, two)
    pair = jnp.stack([jnp.where(first, same, other), jnp.where(first, other, same)])
    pair, grad_image, grad_text = lax.optimization_barrier((pair, grad_image, grad_text))
    across = moved(pair, hop(dz=2))
    ring = [pair, moved(pair, hop(dz=-1)), across, moved(pair, hop(dz=1))]
    ring = jnp.stack(ring + ring, axis=1)
    ring = lax.dynamic_slice_in_dim(ring, 4 - plane, 4, 1)
    ring = ring.reshape(2, columns, width).astype(F32)
    return (grad_image, grad_text, ring[0].T, ring[1].T)


def solution(mesh):
    fine = Mesh(mesh.devices.reshape(SIZES), AXES)
    rows = P(AXES, None)
    cols = P(None, ("yl", "core"))
    return jax.shard_map(
        body,
        mesh=fine,
        in_specs=(rows, rows, cols, cols, P(), P()),
        out_specs=(rows, rows, cols, cols),
        check_vma=False,
    )
```
